256 devices in a mesh: ex: 16 (over z_lo, y), par: 16 (over z_hi, x, core).
Axes of the slice: x: 4, y: 4, z: 8 (z_hi: 2, z_lo: 4; z = z_hi * 4 + z_lo), core: 2. Of those that a mesh axis runs over, the one named last changes fastest.
Arguments:
- inputs: bfloat16 [8192, 4096], P('ex', 'par'), may hold values from -6 to 6
- w_gate: bfloat16 [4096, 11008], P(None, 'par'), may hold values from -0.09375 to 0.09375
- w_up: bfloat16 [4096, 11008], P(None, 'par'), may hold values from -0.09375 to 0.09375
- out_grads: bfloat16 [8192, 4096], P('ex', 'par'), may hold values from -6 to 6
- proj_hidden: bfloat16 [11008, 64], P('par'), may hold values from -0.0546875 to 0.0546875
- proj_model: bfloat16 [4096, 64], P('par'), may hold values from -0.09375 to 0.09375
Outputs:
- features: float32 [256, 4096], P(('ex', 'par'))
- gram: float32 [4096, 4096], P('par')
The draws below stay inside these ranges and needn't reach their ends.
All inputs are finite; a program needn't handle non-finite values.
Results may differ from the reference program's by a relative error of at most 0.022.
Values may be sent and summed in bfloat16 or wider, within the bound.
No kernel may reach another device: no remote copies, remote signals or barrier semaphores. Data moves between devices by JAX's collectives and lax.ppermute only.
A program may use at most 64 MiB of HBM per device.

```python
import jax
import jax.numpy as jnp
from jax import lax

D = 4096
FF = 11008
KA = 64
KB = 64
SEQ = 32
EXAMPLES = 256
TOKENS = 8192


def levels(own_key, extent, split, smallest, largest):
    factor_of, own = 1.0, jax.random.fold_in(own_key, 6)
    for dim, shards_of in split:
        heights = jnp.exp(jax.random.uniform(jax.random.fold_in(own, dim), (shards_of,), jnp.float32, smallest / len(split), largest / len(split)))
        factor_of = factor_of * jnp.repeat(heights, extent[dim] // shards_of).reshape([-1 if axis == dim else 1 for axis in range(len(extent))])
    return factor_of


def bell_draw(own_key, extent, deviation, limit, shards=(), held_as=jnp.bfloat16):
    result = jax.random.normal(own_key, extent, jnp.float32) * deviation
    if len(shards) > 0:
        result = levels(own_key, extent, shards, -0.22, 0.18) * result
    return jnp.clip(result, min=-limit, max=limit).astype(held_as)


def setup_inputs(seed: int = 0) -> dict:
    streams_of = jax.random.split(jax.random.key(seed), 7)
    inputs = bell_draw(streams_of[0], (TOKENS, D), 1.0, 6.0, ((0, 16), (1, 16)))
    w_gate = bell_draw(streams_of[1], (D, FF), D ** -0.5, 0.09375, ((1, 16),))
    w_up = bell_draw(streams_of[2], (D, FF), D ** -0.5, 0.09375, ((1, 16),))
    out_grads = bell_draw(streams_of[3], (TOKENS, D), 1.0, 6.0, ((0, 16), (1, 16)))
    proj_hidden = bell_draw(streams_of[4], (FF, KA), FF ** -0.5, 0.0546875, ((0, 16),))
    proj_model = bell_draw(streams_of[5], (D, KB), D ** -0.5, 0.09375, ((0, 16),))
    return dict(inputs=inputs, w_gate=w_gate, w_up=w_up, out_grads=out_grads, proj_hidden=proj_hidden, proj_model=proj_model)


def reference(inputs, w_gate, w_up, out_grads, proj_hidden, proj_model):
    gate = jnp.dot(inputs, w_gate, preferred_element_type=jnp.float32)
    up = jnp.dot(inputs, w_up, preferred_element_type=jnp.float32)
    hidden = (jax.nn.silu(gate) * up).astype(jnp.bfloat16)
    left = jnp.dot(hidden, proj_hidden, preferred_element_type=jnp.float32)
    right = jnp.dot(out_grads, proj_model, preferred_element_type=jnp.float32)
    left = left.reshape(EXAMPLES, SEQ, KA)
    right = right.reshape(EXAMPLES, SEQ, KB)
    outer = jnp.einsum('eta,etb->eab', left, right, precision=lax.Precision.HIGHEST)
    features = outer.reshape(EXAMPLES, KA * KB) / jnp.sqrt(jnp.float32(SEQ))
    features_bf = features.astype(jnp.bfloat16)
    gram = jnp.dot(features_bf.T, features_bf, preferred_element_type=jnp.float32) / jnp.float32(EXAMPLES)
    return (features, gram)
```

```python
import functools

import jax
import jax.numpy as jnp
from jax import lax
from jax.experimental import pallas as pl
from jax.experimental.pallas import tpu as pltpu
from jax.sharding import PartitionSpec as P

SEQ = 32
BOTH = ("ex", "par")


def pairs(move):
    def index(z, y, x, core):
        z, y, x = z % 8, y % 4, x % 4
        return ((z % 4) * 4 + y) * 16 + (z // 4) * 8 + x * 2 + core

    return [
        (index(z, y, x, c), index(*move(z, y, x, c)))
        for z in range(8)
        for y in range(4)
        for x in range(4)
        for c in range(2)
    ]


def send(value, move):
    return lax.ppermute(value, BOTH, pairs(move))


def shift_x(n):
    return lambda z, y, x, c: (z, y, x + n, c)


def shift_z(n):
    return lambda z, y, x, c: (z + n, y, x, c)


def other_core(z, y, x, c):
    return (z, y, x, 1 - c)


def shift_first(n):
    return lambda z, y, x, c: (z, y + n, x, c) if c == 0 else (z, y, x + n, c)


def shift_second(n):
    return lambda z, y, x, c: (z, y + n, x, c) if c == 1 else (z, y, x + n, c)


def hidden_part(first, rows, units, *refs):
    if first:
        order, side, *blocks = refs[:10]
        gate_w, up_w, gate_out, up_out, held, sems = refs[10:]
    else:
        order, side, *blocks = refs[:10]
        gate_w, up_w, gate_in, up_in, proj, right, out, held, gate_acc, up_acc, sems = refs[10:]
        gate_out, up_out = gate_acc, up_acc
    step = pl.program_id(0)

    def copy(j, s):
        lanes = pl.ds(pl.multiple_of((side[0] if s == 0 else 1 - side[0]) * 256, 256), 256)
        return pltpu.make_async_copy(blocks[2 * j + s], held.at[j, :, lanes], sems.at[j, s])

    @pl.when(step == 0)
    def _():
        for j in range(4):
            for s in range(2):
                copy(j, s).start()

    for j in range(4):

        @pl.when(step == j)
        def _(j=j):
            copy(j, 0).wait()
            copy(j, 1).wait()

    block = held[step]
    dims = (((1,), (1,)), ((), ()))
    gate = lax.dot_general(gate_w[...], block, dims, preferred_element_type=jnp.float32)
    up = lax.dot_general(up_w[...], block, dims, preferred_element_type=jnp.float32)

    @pl.when(step == 0)
    def _():
        if first:
            gate_out[...] = gate
            up_out[...] = up
        else:
            gate_out[...] = gate + gate_in[...]
            up_out[...] = up + up_in[...]

    @pl.when(step > 0)
    def _():
        gate_out[...] += gate
        up_out[...] += up

    if not first:

        @pl.when(step == 3)
        def _():
            value = gate_out[...]
            hidden = (value / (1.0 + jnp.exp(-value)) * up_out[...]).astype(jnp.bfloat16)
            left = jnp.dot(proj[...], hidden, preferred_element_type=jnp.float32)
            out[:, :64] = left.T
            out[:, 64:] = right[...]


def call_part(first, order, side, blocks, w_gate, w_up, rest):
    rows, units = blocks[0].shape[0], w_gate.shape[0]
    weight = pl.BlockSpec((units, 512), lambda k, order, side: (0, order[k]))
    whole = lambda shape: pl.BlockSpec(shape, lambda k, order, side: (0,) * len(shape))
    accs = [jax.ShapeDtypeStruct((units, rows), jnp.float32)] * 2
    out = jax.ShapeDtypeStruct((rows, 128), jnp.float32)
    scratch = [pltpu.VMEM((4, rows, 512), jnp.bfloat16)]
    if not first:
        scratch += [pltpu.VMEM((units, rows), jnp.float32)] * 2
    scratch += [pltpu.SemaphoreType.DMA((4, 2))]
    flops = 2 * 2 * rows * units * 2048
    return pl.pallas_call(
        functools.partial(hidden_part, first, rows, units),
        out_shape=accs if first else out,
        grid_spec=pltpu.PrefetchScalarGridSpec(
            num_scalar_prefetch=2,
            grid=(4,),
            in_specs=[pl.BlockSpec(memory_space=pl.ANY)] * 8 + [weight, weight] + [whole(r.shape) for r in rest],
            out_specs=[whole(a.shape) for a in accs] if first else whole(out.shape),
            scratch_shapes=scratch,
        ),
        compiler_params=pltpu.CompilerParams(vmem_limit_bytes=40 * 1024 * 1024),
        cost_estimate=pl.CostEstimate(flops=flops, bytes_accessed=10_000_000, transcendentals=0),
        name="first_half" if first else "second_half",
    )(order, side, *blocks, w_gate, w_up, *rest)


def on_device(inputs, w_gate, w_up, out_grads, proj_hidden, proj_model):
    rows = inputs.shape[0]
    par = lax.axis_index("par")
    z_hi, x, core = par // 8, (par // 2) % 4, par % 2
    w_gate, w_up, proj = w_gate.T, w_up.T, proj_hidden.T

    far = send(inputs, shift_z(4))
    near = [inputs] + [send(inputs, shift_x(n)) for n in (1, 3, 2)]
    near_all = [b for n in near for b in (n, send(n, other_core))]
    far = [far] + [send(far, shift_x(n)) for n in (1, 3, 2)]
    far_all = [b for n in far for b in (n, send(n, other_core))]
    from_x = jnp.stack([x, (x + 3) % 4, (x + 1) % 4, (x + 2) % 4]).astype(jnp.int32)
    side = core.astype(jnp.int32).reshape(1)

    right = jnp.dot(out_grads, proj_model, preferred_element_type=jnp.float32)
    accs = call_part(True, z_hi * 4 + from_x, side, near_all, w_gate, w_up, [])
    both = call_part(False, (1 - z_hi) * 4 + from_x, side, far_all, w_gate, w_up, [*accs, proj, right])

    both = both.reshape(2, 4, 2, SEQ, 128)
    pick = lambda v, i, axis: lax.dynamic_index_in_dim(v, i, axis, keepdims=False)
    both = pick(both, core, 2) + send(pick(both, 1 - core, 2), other_core)
    part = pick(both, x, 1)
    for n in (1, 3, 2):
        part = part + send(pick(both, (x + n) % 4, 1), shift_x(n))

    part = part.astype(jnp.bfloat16)
    along = [part] + [send(part, shift_z(n)) for n in range(1, 8)]
    total = jnp.stack([along[n].astype(jnp.float32) + along[n + 4].astype(jnp.float32) for n in range(4)])
    total = total.reshape(8, SEQ, 128)
    outer = jnp.einsum("eta,etb->eab", total[..., :64], total[..., 64:], precision=lax.Precision.HIGHEST)
    feats = outer.reshape(8, 4096) / jnp.sqrt(jnp.float32(SEQ))
    features = lax.dynamic_slice_in_dim(feats, z_hi, 1, 0)

    feats = feats.astype(jnp.bfloat16)
    feats = jnp.concatenate([feats] + [send(feats, shift_first(n)) for n in (1, 3, 2)])
    feats = jnp.concatenate([feats] + [send(feats, shift_second(n)) for n in (1, 3, 2)])
    feats = jnp.concatenate([feats, send(feats, other_core)])
    mine = lax.dynamic_slice_in_dim(feats, par * 256, 256, 1)
    gram = jnp.dot(mine.T, feats, preferred_element_type=jnp.float32) * (1.0 / 256)
    return (features, gram)


def solution(mesh):
    placed = (
        P("ex", "par"),
        P(None, "par"),
        P(None, "par"),
        P("ex", "par"),
        P("par", None),
        P("par", None),
    )
    return jax.shard_map(
        on_device,
        mesh=mesh,
        in_specs=placed,
        out_specs=(P(("ex", "par"), None), P("par", None)),
        check_vma=False,
    )
```

```python
import functools

import jax
import jax.numpy as jnp
from jax import lax
from jax.experimental import pallas as pl
from jax.experimental.pallas import tpu as pltpu
from jax.sharding import PartitionSpec as P

SEQ = 32
BOTH = ("ex", "par")


def pairs(move):
    def index(z, y, x, core):
        z, y, x = z % 8, y % 4, x % 4
        return ((z % 4) * 4 + y) * 16 + (z // 4) * 8 + x * 2 + core

    return [
        (index(z, y, x, c), index(*move(z, y, x, c)))
        for z in range(8)
        for y in range(4)
        for x in range(4)
        for c in range(2)
    ]


def send(value, move):
    return lax.ppermute(value, BOTH, pairs(move))


def shift_x(n):
    return lambda z, y, x, c: (z, y, x + n, c)


def shift_z(n):
    return lambda z, y, x, c: (z + n, y, x, c)


def other_core(z, y, x, c):
    return (z, y, x, 1 - c)


VMEM = pltpu.VMEM
ROWS_TIMES_ROWS = (((1,), (1,)), ((), ()))
LINES = [[(z % 4 * 4 + y) * 16 + z // 4 * 8 + n for z in range(8)] for y in range(4) for n in range(8)]
PLANES = [
    [(z % 4 * 4 + y) * 16 + z // 4 * 8 + x * 2 + c for x in range(4) for y in range(4)]
    for z in range(8)
    for c in range(2)
]


def block_copies(blocks, held, sems):
    return [
        pltpu.make_async_copy(v, held.at[:, pl.ds(n * 256, 256)], sems.at[n // 2, n % 2]) for n, v in enumerate(blocks)
    ]


def weight_copies(starts, first, count, gate, up, weights, sems):
    units, made = gate.shape[0], []
    for n in range(2 * count):
        cols = pl.ds(pl.multiple_of(starts[first + n], 256), 256)
        for m, source in enumerate((gate, up)):
            to = weights.at[pl.ds(m * units, units), pl.ds(n * 256, 256)]
            made.append(pltpu.make_async_copy(source.at[:, cols], to, sems.at[n // 2, 2 + n % 2 * 2 + m]))
    return made


def start(copies):
    for c in copies:
        c.start()


def wait(copies):
    for c in copies:
        c.wait()


def product(weights, held, j):
    cols = slice(j * 512, (j + 1) * 512)
    return lax.dot_general(weights[:, cols], held[:, cols], ROWS_TIMES_ROWS, preferred_element_type=jnp.float32)


def own_kernel(starts, second, first, gate, up, out, held, weights, sems):
    copies = weight_copies(starts, 0, 1, gate, up, weights, sems) + block_copies((first, second), held, sems)
    start(copies)
    wait(copies)
    out[...] = product(weights, held, 0)


def near_kernel(starts, *refs):
    blocks, (gate, up, near, out, held, weights, sems) = refs[:6], refs[6:]
    loads = block_copies(blocks, held, sems)
    columns = weight_copies(starts, 2, 3, gate, up, weights, sems)
    start(loads)
    start(columns)
    for j in range(3):
        wait(loads[2 * j : 2 * j + 2])
        wait(columns[4 * j : 4 * j + 4])
        if j == 0:
            out[...] = product(weights, held, 0) + near[...]
        else:
            out[...] += product(weights, held, j)


def middle_kernel(starts, gate, up, grads, proj_model, *refs):
    blocks, (near, out, later, right, weights, sems) = refs[:6], refs[6:]
    columns = weight_copies(starts, 8, 3, gate, up, weights, sems)
    later_columns = weight_copies(starts, 14, 1, gate, up, later, sems.at[pl.ds(3, 1)])
    start(columns)
    start(later_columns)
    right[...] = lax.dot_general(grads[...], proj_model[...], ROWS_TIMES_ROWS, preferred_element_type=jnp.float32)
    for j in range(3):
        held = jnp.concatenate([blocks[2 * j][...], blocks[2 * j + 1][...]], axis=1)
        wait(columns[4 * j : 4 * j + 4])
        value = lax.dot_general(
            weights[:, j * 512 : (j + 1) * 512], held, ROWS_TIMES_ROWS, preferred_element_type=jnp.float32
        )
        if j == 0:
            out[...] = value + near[...]
        else:
            out[...] += value
    wait(later_columns)


def last_kernel(proj, first, second, weights, sums, right, out):
    units = proj.shape[1]
    held = jnp.concatenate([first[...], second[...]], axis=1)
    value = lax.dot_general(weights[...], held, ROWS_TIMES_ROWS, preferred_element_type=jnp.float32)
    value = value + sums[...]
    gate, up = value[:units], value[units:]
    hidden = (gate / (1.0 + jnp.exp(-gate)) * up).astype(jnp.bfloat16)
    left = jnp.dot(proj[...], hidden, preferred_element_type=jnp.float32)
    out[:, :64] = left.T
    out[:, 64:] = right[...]


def call(kernel, name, out, flops, scalars, anywhere, in_hbm, copied, in_vmem, scratch):
    vmem = pl.BlockSpec(memory_space=VMEM)
    return pl.pallas_call(
        kernel,
        out_shape=[VMEM(shape, dtype) for shape, dtype in out],
        in_specs=[pl.BlockSpec(memory_space=pltpu.SMEM)] * len(scalars)
        + [pl.BlockSpec(memory_space=pl.ANY)] * len(anywhere)
        + [pl.BlockSpec(memory_space=pltpu.HBM)] * len(in_hbm)
        + [vmem] * (len(copied) + len(in_vmem)),
        out_specs=[vmem] * len(out),
        scratch_shapes=scratch,
        compiler_params=pltpu.CompilerParams(vmem_limit_bytes=24 * 1024 * 1024),
        cost_estimate=pl.CostEstimate(flops=flops, bytes_accessed=0, transcendentals=0),
        name=name,
    )(
        *scalars,
        *anywhere,
        *[pltpu.with_memory_space_constraint(v, pltpu.HBM) for v in in_hbm],
        *copied,
        *[pltpu.with_memory_space_constraint(v, VMEM) for v in in_vmem],
    )


def on_device(inputs, w_gate, w_up, out_grads, proj_hidden, proj_model):
    rows, units = inputs.shape[0], w_gate.shape[1]
    par = lax.axis_index("par")
    z_hi, x, core = par // 8, (par // 2) % 4, par % 2

    far = send(inputs, shift_z(4))
    sibling = send(inputs, other_core)
    own, sibling = lax.optimization_barrier((inputs, sibling))
    by_x = [send(own, shift_x(n)) for n in (1, 3, 2)]

    chips = jnp.stack([x, (x + 3) % 4, (x + 1) % 4, (x + 2) % 4])
    cores = jnp.stack([core, 1 - core])
    starts = jnp.stack([z_hi, 1 - z_hi])[:, None, None] * 2048 + chips[:, None] * 512 + cores * 256
    starts = starts.reshape(16).astype(jnp.int32)
    w_gate, w_up = w_gate.T, w_up.T
    sums_type, bf16 = ((2 * units, rows), jnp.float32), jnp.bfloat16
    held = lambda n: VMEM((rows, n * 512), bf16)
    columns = lambda n: VMEM((2 * units, n * 512), bf16)
    sems = pltpu.SemaphoreType.DMA((3, 6))
    flops = 4 * rows * units * 512
    (sums,) = call(
        own_kernel,
        "own",
        [sums_type],
        flops,
        [starts],
        [sibling],
        [inputs, w_gate, w_up],
        [],
        [],
        [held(1), columns(1), sems],
    )
    far, sums = lax.optimization_barrier((far, sums))
    far = [far] + [send(far, shift_x(n)) for n in (1, 3, 2)]
    *by_x, _ = lax.optimization_barrier((*by_x, far[0]))
    near_all = [b for n in by_x for b in (n, send(n, other_core))]
    (sums,) = call(
        near_kernel,
        "near",
        [sums_type],
        0,
        [starts],
        [],
        near_all + [w_gate, w_up],
        [],
        [sums],
        [held(3), columns(3), sems],
    )
    *by_x, sums = lax.optimization_barrier((*far[1:], sums))
    far_all = [b for n in (far[0], *by_x) for b in (n, send(n, other_core))]
    sums, weights, right = call(
        middle_kernel,
        "middle",
        [sums_type, ((2 * units, 512), bf16), ((rows, 64), jnp.float32)],
        3 * flops,
        [starts],
        [],
        [w_gate, w_up],
        [out_grads, proj_model.T],
        [*far_all[:6], sums],
        [columns(3), pltpu.SemaphoreType.DMA((4, 6))],
    )
    (both,) = call(
        last_kernel,
        "last",
        [((rows, 128), jnp.float32)],
        flops,
        [],
        [],
        [],
        [proj_hidden.T],
        [*far_all[6:], weights, sums, right],
        [],
    )

    both = both.reshape(2, 4, 2, SEQ, 128)
    pick = lambda v, i, axis: lax.dynamic_index_in_dim(v, i, axis, keepdims=False)
    both = pick(both, core, 2) + send(pick(both, 1 - core, 2), other_core)
    part = pick(both, x, 1)
    for n in (1, 3, 2):
        part = part + send(pick(both, (x + n) % 4, 1), shift_x(n))

    part = jnp.broadcast_to(part.astype(jnp.bfloat16), (8, *part.shape))
    along = lax.all_to_all(part, BOTH, 0, 0, axis_index_groups=LINES).astype(jnp.float32)
    total = (along[:4] + along[4:]).reshape(8, SEQ, 128)
    outer = jnp.einsum("eta,etb->eab", total[..., :64], total[..., 64:], precision=lax.Precision.HIGHEST)
    feats = outer.reshape(8, 4096) / jnp.sqrt(jnp.float32(SEQ))
    z_lo = lax.axis_index("ex") // 4
    features = lax.dynamic_slice_in_dim(feats, z_lo * 2 + z_hi, 1, 0)

    feats = jnp.broadcast_to(feats.astype(jnp.bfloat16), (16, 8, 4096))
    feats = lax.all_to_all(feats, BOTH, 0, 0, axis_index_groups=PLANES).reshape(128, 4096)
    feats = jnp.concatenate([feats, send(feats, other_core)])
    mine = lax.dynamic_slice_in_dim(feats, par * 256, 256, 1)
    gram = jnp.dot(mine.T, feats, preferred_element_type=jnp.float32) * (1.0 / 256)
    return (features, gram)


def solution(mesh):
    placed = (
        P("ex", "par"),
        P(None, "par"),
        P(None, "par"),
        P("ex", "par"),
        P("par", None),
        P("par", None),
    )
    return jax.shard_map(
        on_device,
        mesh=mesh,
        in_specs=placed,
        out_specs=(P(("ex", "par"), None), P("par", None)),
        check_vma=False,
    )
```

```python
import functools

import jax
import jax.numpy as jnp
from jax import lax
from jax.experimental import pallas as pl
from jax.experimental.pallas import tpu as pltpu
from jax.sharding import PartitionSpec as P

SEQ = 32
BOTH = ("ex", "par")


def pairs(move):
    def index(z, y, x, core):
        z, y, x = z % 8, y % 4, x % 4
        return ((z % 4) * 4 + y) * 16 + (z // 4) * 8 + x * 2 + core

    return [
        (index(z, y, x, c), index(*move(z, y, x, c)))
        for z in range(8)
        for y in range(4)
        for x in range(4)
        for c in range(2)
    ]


def send(value, move):
    return lax.ppermute(value, BOTH, pairs(move))


def shift_x(n):
    return lambda z, y, x, c: (z, y, x + n, c)


def shift_z(n):
    return lambda z, y, x, c: (z + n, y, x, c)


def other_core(z, y, x, c):
    return (z, y, x, 1 - c)


VMEM = pltpu.VMEM
ROWS_TIMES_ROWS = (((1,), (1,)), ((), ()))
LINES = [[(z % 4 * 4 + y) * 16 + z // 4 * 8 + n for z in range(8)] for y in range(4) for n in range(8)]
PLANES = [
    [(z % 4 * 4 + y) * 16 + z // 4 * 8 + x * 2 + c for x in range(4) for y in range(4)]
    for z in range(8)
    for c in range(2)
]


PARTS = ((0, 1), (1, 3), (4, 3), (7, 1))


def stage_kernel(starts, inputs, gate, up, held, *refs):
    outs, sem, sems = refs[:4], refs[4], refs[5]
    units = gate.shape[0]
    copies = [pltpu.make_async_copy(inputs, held, sem)]
    for out, (first, count) in zip(outs, PARTS):
        for n in range(2 * count):
            cols = pl.ds(pl.multiple_of(starts[2 * first + n], 256), 256)
            for m, source in enumerate((gate, up)):
                to = out.at[pl.ds(m * units, units), pl.ds(n * 256, 256)]
                copies.append(pltpu.make_async_copy(source.at[:, cols], to, sems.at[2 * first + n, m]))
    for c in copies:
        c.start()
    for c in copies:
        c.wait()


def product(weights, j, first, second):
    held = jnp.concatenate([first[...], second[...]], axis=1)
    cols = weights[:, j * 512 : (j + 1) * 512]
    return lax.dot_general(cols, held, ROWS_TIMES_ROWS, preferred_element_type=jnp.float32)


def own_kernel(first, second, weights, out):
    out[...] = product(weights, 0, first, second)


def three_chips(blocks, weights, near, out):
    out[...] = product(weights, 0, *blocks[:2]) + near[...]
    for j in range(1, 3):
        out[...] += product(weights, j, *blocks[2 * j : 2 * j + 2])


def near_kernel(*refs):
    blocks, (weights, near, out) = refs[:6], refs[6:]
    three_chips(blocks, weights, near, out)


def middle_kernel(grads, proj_model, *refs):
    blocks, (weights, near, out, right) = refs[:6], refs[6:]
    right[...] = lax.dot_general(grads[...], proj_model[...], ROWS_TIMES_ROWS, preferred_element_type=jnp.float32)
    three_chips(blocks, weights, near, out)


def last_kernel(starts, proj, first, second, weights, sums, right, keep, give, whole):
    units = proj.shape[1]
    value = product(weights, 0, first, second) + sums[...]
    gate, up = value[:units], value[units:]
    hidden = (gate / (1.0 + jnp.exp(-gate)) * up).astype(jnp.bfloat16)
    left = jnp.dot(proj[...], hidden, preferred_element_type=jnp.float32)
    whole[:, :64] = left.T
    whole[:, 64:] = right[...]
    par = starts[16]
    core, x = lax.rem(par, 2), lax.rem(par // 2, 4)
    for n in range(4):
        for z_hi in range(2):
            first_row = (z_hi * 4 + lax.rem(x + n, 4)) * 2 * SEQ
            for out, side in ((keep, core), (give, 1 - core)):
                rows = pl.ds(pl.multiple_of(first_row + side * SEQ, SEQ), SEQ)
                out[n, z_hi] = whole[rows]


def call(kernel, name, out, flops, scalars, anywhere, in_hbm, copied, in_vmem, scratch):
    vmem = pl.BlockSpec(memory_space=VMEM)
    return pl.pallas_call(
        kernel,
        out_shape=[VMEM(shape, dtype) for shape, dtype in out],
        in_specs=[pl.BlockSpec(memory_space=pltpu.SMEM)] * len(scalars)
        + [pl.BlockSpec(memory_space=pl.ANY)] * len(anywhere)
        + [pl.BlockSpec(memory_space=pltpu.HBM)] * len(in_hbm)
        + [vmem] * (len(copied) + len(in_vmem)),
        out_specs=[vmem] * len(out),
        scratch_shapes=scratch,
        compiler_params=pltpu.CompilerParams(vmem_limit_bytes=16 * 1024 * 1024),
        cost_estimate=pl.CostEstimate(flops=flops, bytes_accessed=0, transcendentals=0),
        name=name,
    )(
        *scalars,
        *anywhere,
        *[pltpu.with_memory_space_constraint(v, pltpu.HBM) for v in in_hbm],
        *copied,
        *[pltpu.with_memory_space_constraint(v, VMEM) for v in in_vmem],
    )


def on_device(inputs, w_gate, w_up, out_grads, proj_hidden, proj_model):
    rows, units = inputs.shape[0], w_gate.shape[1]
    par, ex = lax.axis_index("par"), lax.axis_index("ex")
    z_hi, x, core = par // 8, (par // 2) % 4, par % 2

    far = send(inputs, shift_z(4))
    sibling = send(inputs, other_core)
    own, sibling = lax.optimization_barrier((inputs, sibling))
    by_x = [send(own, shift_x(n)) for n in (2, 1, 3)]
    by_x = by_x[1:] + by_x[:1]

    chips = jnp.stack([x, (x + 3) % 4, (x + 1) % 4, (x + 2) % 4])
    cores = jnp.stack([core, 1 - core])
    starts = jnp.stack([z_hi, 1 - z_hi])[:, None, None] * 2048 + chips[:, None] * 512 + cores * 256
    starts = jnp.concatenate([starts.reshape(16), jnp.stack([par, ex])]).astype(jnp.int32)
    w_gate, w_up = w_gate.T, w_up.T
    sums_type, bf16 = ((2 * units, rows), jnp.float32), jnp.bfloat16
    flops = 4 * rows * units * 512
    held, *weights = call(
        stage_kernel,
        "stage",
        [((rows, 256), bf16)] + [((2 * units, 512 * count), bf16) for _, count in PARTS],
        0,
        [starts],
        [],
        [inputs, w_gate, w_up],
        [],
        [],
        [pltpu.SemaphoreType.DMA(()), pltpu.SemaphoreType.DMA((16, 2))],
    )
    far, sibling, held, *weights = lax.optimization_barrier((far, sibling, held, *weights))
    (sums,) = call(own_kernel, "own", [sums_type], flops, [], [], [], [], [held, sibling, weights[0]], [])
    far = [far] + [send(far, shift_x(n)) for n in (1, 3, 2)]
    *by_x, _ = lax.optimization_barrier((*by_x, far[0]))
    near_all = [b for n in by_x for b in (n, send(n, other_core))]
    (sums,) = call(
        near_kernel, "near", [sums_type], 3 * flops, [], [], [], [], [*near_all, weights[1], sums], []
    )
    far[1], far[2], sums = lax.optimization_barrier((far[1], far[2], sums))
    far_all = [b for n in far for b in (n, send(n, other_core))]
    sums, right = call(
        middle_kernel,
        "middle",
        [sums_type, ((rows, 64), jnp.float32)],
        3 * flops,
        [],
        [],
        [],
        [out_grads, proj_model.T],
        [*far_all[:6], weights[2], sums],
        [],
    )
    keep, give = call(
        last_kernel,
        "last",
        [((4, 2, SEQ, 128), jnp.float32)] * 2,
        flops,
        [starts],
        [],
        [],
        [proj_hidden.T],
        [*far_all[6:], weights[3], sums, right],
        [VMEM((rows, 128), jnp.float32)],
    )
    keep, give, par, ex = lax.optimization_barrier((keep, give, par, ex))

    keep = keep + send(give, other_core)
    part = keep[0] + sum(send(keep[n], shift_x(n)) for n in (1, 3, 2))

    part = jnp.broadcast_to(part.astype(jnp.bfloat16), (8, *part.shape))
    along = lax.all_to_all(part, BOTH, 0, 0, axis_index_groups=LINES).astype(jnp.float32)
    total = (along[:4] + along[4:]).reshape(8, SEQ, 128)
    outer = jnp.einsum("eta,etb->eab", total[..., :64], total[..., 64:], precision=lax.Precision.HIGHEST)
    feats = outer.reshape(8, 4096) / jnp.sqrt(jnp.float32(SEQ))
    features = lax.dynamic_slice_in_dim(feats, ex // 4 * 2 + par // 8, 1, 0)

    feats = jnp.broadcast_to(feats.astype(jnp.bfloat16), (16, 8, 4096))
    feats = lax.all_to_all(feats, BOTH, 0, 0, axis_index_groups=PLANES).reshape(128, 4096)
    feats = jnp.concatenate([feats, send(feats, other_core)])
    mine = lax.dynamic_slice_in_dim(feats, par * 256, 256, 1)
    gram = jnp.dot(mine.T, feats, preferred_element_type=jnp.float32) * (1.0 / 256)
    return (features, gram)


def solution(mesh):
    placed = (
        P("ex", "par"),
        P(None, "par"),
        P(None, "par"),
        P("ex", "par"),
        P("par", None),
        P("par", None),
    )
    return jax.shard_map(
        on_device,
        mesh=mesh,
        in_specs=placed,
        out_specs=(P(("ex", "par"), None), P("par", None)),
        check_vma=False,
    )
```

```python
import functools

import jax
import jax.numpy as jnp
from jax import lax
from jax.experimental import pallas as pl
from jax.experimental.pallas import tpu as pltpu
from jax.sharding import PartitionSpec as P

SEQ = 32
BOTH = ("ex", "par")


def pairs(move):
    def index(z, y, x, core):
        z, y, x = z % 8, y % 4, x % 4
        return ((z % 4) * 4 + y) * 16 + (z // 4) * 8 + x * 2 + core

    return [
        (index(z, y, x, c), index(*move(z, y, x, c)))
        for z in range(8)
        for y in range(4)
        for x in range(4)
        for c in range(2)
    ]


def send(value, move):
    return lax.ppermute(value, BOTH, pairs(move))


def shift_x(n):
    return lambda z, y, x, c: (z, y, x + n, c)


def shift_z(n):
    return lambda z, y, x, c: (z + n, y, x, c)


def other_core(z, y, x, c):
    return (z, y, x, 1 - c)


VMEM = pltpu.VMEM
ROWS_TIMES_ROWS = (((1,), (1,)), ((), ()))
LINES = [[(z % 4 * 4 + y) * 16 + z // 4 * 8 + n for z in range(8)] for y in range(4) for n in range(8)]
SQUARES = [[(z % 4 * 4 + y) * 16 + z // 4 * 8 + n for n in range(8)] for z in range(8) for y in range(4)]
PLANES = [
    [(z % 4 * 4 + y) * 16 + z // 4 * 8 + x * 2 + c for x in range(4) for y in range(4)]
    for z in range(8)
    for c in range(2)
]


PARTS = ((0, 1), (1, 3), (4, 3), (7, 1))


def stage_kernel(starts, inputs, gate, up, held, *refs):
    outs, sem, sems = refs[:4], refs[4], refs[5]
    units = gate.shape[0]
    copies = [pltpu.make_async_copy(inputs, held, sem)]
    for out, (first, count) in zip(outs, PARTS):
        for n in range(2 * count):
            cols = pl.ds(pl.multiple_of(starts[2 * first + n], 256), 256)
            for m, source in enumerate((gate, up)):
                to = out.at[pl.ds(m * units, units), pl.ds(n * 256, 256)]
                copies.append(pltpu.make_async_copy(source.at[:, cols], to, sems.at[2 * first + n, m]))
    for c in copies:
        c.start()
    for c in copies:
        c.wait()


def product(weights, j, first, second):
    held = jnp.concatenate([first[...], second[...]], axis=1)
    cols = weights[:, j * 512 : (j + 1) * 512]
    return lax.dot_general(cols, held, ROWS_TIMES_ROWS, preferred_element_type=jnp.float32)


def own_kernel(first, second, weights, out):
    out[...] = product(weights, 0, first, second)


def three_chips(blocks, weights, near, out):
    out[...] = product(weights, 0, *blocks[:2]) + near[...]
    for j in range(1, 3):
        out[...] += product(weights, j, *blocks[2 * j : 2 * j + 2])


def near_kernel(*refs):
    blocks, (weights, near, out) = refs[:6], refs[6:]
    three_chips(blocks, weights, near, out)


def middle_kernel(grads, proj_model, *refs):
    blocks, (weights, near, out, right) = refs[:6], refs[6:]
    right[...] = lax.dot_general(grads[...], proj_model[...], ROWS_TIMES_ROWS, preferred_element_type=jnp.float32)
    three_chips(blocks, weights, near, out)


def last_kernel(proj, first, second, weights, sums, right, out, whole):
    units = proj.shape[1]
    value = product(weights, 0, first, second) + sums[...]
    gate, up = value[:units], value[units:]
    hidden = (gate / (1.0 + jnp.exp(-gate)) * up).astype(jnp.bfloat16)
    left = jnp.dot(proj[...], hidden, preferred_element_type=jnp.float32)
    whole[:, :64] = left.T
    whole[:, 64:] = right[...]
    for owner in range(8):
        for z_hi in range(2):
            first_row = (z_hi * 8 + owner) * SEQ
            out[owner, z_hi] = whole[first_row : first_row + SEQ].astype(out.dtype)


def call(kernel, name, out, flops, scalars, anywhere, in_hbm, copied, in_vmem, scratch):
    vmem = pl.BlockSpec(memory_space=VMEM)
    return pl.pallas_call(
        kernel,
        out_shape=[VMEM(shape, dtype) for shape, dtype in out],
        in_specs=[pl.BlockSpec(memory_space=pltpu.SMEM)] * len(scalars)
        + [pl.BlockSpec(memory_space=pl.ANY)] * len(anywhere)
        + [pl.BlockSpec(memory_space=pltpu.HBM)] * len(in_hbm)
        + [vmem] * (len(copied) + len(in_vmem)),
        out_specs=[vmem] * len(out),
        scratch_shapes=scratch,
        compiler_params=pltpu.CompilerParams(vmem_limit_bytes=16 * 1024 * 1024),
        cost_estimate=pl.CostEstimate(flops=flops, bytes_accessed=0, transcendentals=0),
        name=name,
    )(
        *scalars,
        *anywhere,
        *[pltpu.with_memory_space_constraint(v, pltpu.HBM) for v in in_hbm],
        *copied,
        *[pltpu.with_memory_space_constraint(v, VMEM) for v in in_vmem],
    )


def on_device(inputs, w_gate, w_up, out_grads, proj_hidden, proj_model):
    rows, units = inputs.shape[0], w_gate.shape[1]
    par, ex = lax.axis_index("par"), lax.axis_index("ex")
    z_hi, x, core = par // 8, (par // 2) % 4, par % 2

    far = send(inputs, shift_z(4))
    sibling = send(inputs, other_core)
    own, sibling = lax.optimization_barrier((inputs, sibling))
    by_x = [send(own, shift_x(n)) for n in (2, 1, 3)]
    by_x = by_x[1:] + by_x[:1]

    chips = jnp.stack([x, (x + 3) % 4, (x + 1) % 4, (x + 2) % 4])
    cores = jnp.stack([core, 1 - core])
    starts = jnp.stack([z_hi, 1 - z_hi])[:, None, None] * 2048 + chips[:, None] * 512 + cores * 256
    starts = jnp.concatenate([starts.reshape(16), jnp.stack([par, ex])]).astype(jnp.int32)
    w_gate, w_up = w_gate.T, w_up.T
    sums_type, bf16 = ((2 * units, rows), jnp.float32), jnp.bfloat16
    flops = 4 * rows * units * 512
    held, *weights = call(
        stage_kernel,
        "stage",
        [((rows, 256), bf16)] + [((2 * units, 512 * count), bf16) for _, count in PARTS],
        0,
        [starts],
        [],
        [inputs, w_gate, w_up],
        [],
        [],
        [pltpu.SemaphoreType.DMA(()), pltpu.SemaphoreType.DMA((16, 2))],
    )
    far, sibling, held, *weights = lax.optimization_barrier((far, sibling, held, *weights))
    (sums,) = call(own_kernel, "own", [sums_type], flops, [], [], [], [], [held, sibling, weights[0]], [])
    far = [far] + [send(far, shift_x(n)) for n in (1, 3, 2)]
    *by_x, _ = lax.optimization_barrier((*by_x, far[0]))
    near_all = [b for n in by_x for b in (n, send(n, other_core))]
    (sums,) = call(
        near_kernel, "near", [sums_type], 3 * flops, [], [], [], [], [*near_all, weights[1], sums], []
    )
    far[3], sums = lax.optimization_barrier((far[3], sums))
    far_all = [b for n in far for b in (n, send(n, other_core))]
    sums, right = call(
        middle_kernel,
        "middle",
        [sums_type, ((rows, 64), jnp.float32)],
        3 * flops,
        [],
        [],
        [],
        [out_grads, proj_model.T],
        [*far_all[:6], weights[2], sums],
        [],
    )
    (shares,) = call(
        last_kernel,
        "last",
        [((8, 2, SEQ, 128), bf16)],
        flops,
        [],
        [],
        [],
        [proj_hidden.T],
        [*far_all[6:], weights[3], sums, right],
        [VMEM((rows, 128), jnp.float32)],
    )
    shares, par, ex = lax.optimization_barrier((shares, par, ex))

    shares = lax.all_to_all(shares, BOTH, 0, 0, axis_index_groups=SQUARES)
    part = jnp.sum(shares.astype(jnp.float32), axis=0)

    part = jnp.broadcast_to(part.astype(jnp.bfloat16), (8, *part.shape))
    along = lax.all_to_all(part, BOTH, 0, 0, axis_index_groups=LINES).astype(jnp.float32)
    total = (along[:4] + along[4:]).reshape(8, SEQ, 128)
    outer = jnp.einsum("eta,etb->eab", total[..., :64], total[..., 64:], precision=lax.Precision.HIGHEST)
    feats = outer.reshape(8, 4096) / jnp.sqrt(jnp.float32(SEQ))
    features = lax.dynamic_slice_in_dim(feats, ex // 4 * 2 + par // 8, 1, 0)

    feats = jnp.broadcast_to(feats.astype(jnp.bfloat16), (16, 8, 4096))
    feats = lax.all_to_all(feats, BOTH, 0, 0, axis_index_groups=PLANES).reshape(128, 4096)
    feats = jnp.concatenate([feats, send(feats, other_core)])
    mine = lax.dynamic_slice_in_dim(feats, par * 256, 256, 1)
    gram = jnp.dot(mine.T, feats, preferred_element_type=jnp.float32) * (1.0 / 256)
    return (features, gram)


def solution(mesh):
    placed = (
        P("ex", "par"),
        P(None, "par"),
        P(None, "par"),
        P("ex", "par"),
        P("par", None),
        P("par", None),
    )
    return jax.shard_map(
        on_device,
        mesh=mesh,
        in_specs=placed,
        out_specs=(P(("ex", "par"), None), P("par", None)),
        check_vma=False,
    )
```

```python
import functools

import jax
import jax.numpy as jnp
from jax import lax
from jax.experimental import pallas as pl
from jax.experimental.pallas import tpu as pltpu
from jax.sharding import PartitionSpec as P

SEQ = 32
BOTH = ("ex", "par")


def pairs(move):
    def index(z, y, x, core):
        z, y, x = z % 8, y % 4, x % 4
        return ((z % 4) * 4 + y) * 16 + (z // 4) * 8 + x * 2 + core

    return [
        (index(z, y, x, c), index(*move(z, y, x, c)))
        for z in range(8)
        for y in range(4)
        for x in range(4)
        for c in range(2)
    ]


def send(value, move):
    return lax.ppermute(value, BOTH, pairs(move))


def shift_x(n):
    return lambda z, y, x, c: (z, y, x + n, c)


def shift_z(n):
    return lambda z, y, x, c: (z + n, y, x, c)


def other_core(z, y, x, c):
    return (z, y, x, 1 - c)


VMEM = pltpu.VMEM
ROWS_TIMES_ROWS = (((1,), (1,)), ((), ()))
LINES = [[(z % 4 * 4 + y) * 16 + z // 4 * 8 + n for z in range(8)] for y in range(4) for n in range(8)]
SQUARES = [[(z % 4 * 4 + y) * 16 + z // 4 * 8 + n for n in range(8)] for z in range(8) for y in range(4)]
SPIRAL = [(x, (x + y) % 4) for y in range(4) for x in range(4)]
PLANES = [
    [(z % 4 * 4 + y) * 16 + z // 4 * 8 + x * 2 + c for x, y in SPIRAL]
    for z in range(8)
    for c in range(2)
]


PARTS = ((0, 1), (1, 3), (4, 3), (7, 1))


def stage_kernel(starts, inputs, gate, up, held, *refs):
    outs, sem, sems = refs[:4], refs[4], refs[5]
    units = gate.shape[0]
    copies = [pltpu.make_async_copy(inputs, held, sem)]
    for out, (first, count) in zip(outs, PARTS):
        for n in range(2 * count):
            cols = pl.ds(pl.multiple_of(starts[2 * first + n], 256), 256)
            for m, source in enumerate((gate, up)):
                to = out.at[pl.ds(m * units, units), pl.ds(n * 256, 256)]
                copies.append(pltpu.make_async_copy(source.at[:, cols], to, sems.at[2 * first + n, m]))
    for c in copies:
        c.start()
    for c in copies:
        c.wait()


def product(weights, j, first, second):
    held = jnp.concatenate([first[...], second[...]], axis=1)
    cols = weights[:, j * 512 : (j + 1) * 512]
    return lax.dot_general(cols, held, ROWS_TIMES_ROWS, preferred_element_type=jnp.float32)


def own_kernel(first, second, weights, out):
    out[...] = product(weights, 0, first, second)


def three_chips(blocks, weights, near, out):
    out[...] = product(weights, 0, *blocks[:2]) + near[...]
    for j in range(1, 3):
        out[...] += product(weights, j, *blocks[2 * j : 2 * j + 2])


def near_kernel(*refs):
    blocks, (weights, near, out) = refs[:6], refs[6:]
    three_chips(blocks, weights, near, out)


def middle_kernel(grads, proj_model, *refs):
    blocks, (weights, near, out, right) = refs[:6], refs[6:]
    right[...] = lax.dot_general(grads[...], proj_model[...], ROWS_TIMES_ROWS, preferred_element_type=jnp.float32)
    three_chips(blocks, weights, near, out)


def last_kernel(proj, first, second, weights, sums, right, out, whole):
    units = proj.shape[1]
    value = product(weights, 0, first, second) + sums[...]
    gate, up = value[:units], value[units:]
    hidden = (gate / (1.0 + jnp.exp(-gate)) * up).astype(jnp.bfloat16)
    left = jnp.dot(proj[...], hidden, preferred_element_type=jnp.float32)
    whole[:, :64] = left.T
    whole[:, 64:] = right[...]
    for owner in range(8):
        for z_hi in range(2):
            first_row = (z_hi * 8 + owner) * SEQ
            out[owner, z_hi] = whole[first_row : first_row + SEQ].astype(out.dtype)


def call(kernel, name, out, flops, scalars, anywhere, in_hbm, copied, in_vmem, scratch):
    vmem = pl.BlockSpec(memory_space=VMEM)
    return pl.pallas_call(
        kernel,
        out_shape=[VMEM(shape, dtype) for shape, dtype in out],
        in_specs=[pl.BlockSpec(memory_space=pltpu.SMEM)] * len(scalars)
        + [pl.BlockSpec(memory_space=pl.ANY)] * len(anywhere)
        + [pl.BlockSpec(memory_space=pltpu.HBM)] * len(in_hbm)
        + [vmem] * (len(copied) + len(in_vmem)),
        out_specs=[vmem] * len(out),
        scratch_shapes=scratch,
        compiler_params=pltpu.CompilerParams(vmem_limit_bytes=16 * 1024 * 1024),
        cost_estimate=pl.CostEstimate(flops=flops, bytes_accessed=0, transcendentals=0),
        name=name,
    )(
        *scalars,
        *anywhere,
        *[pltpu.with_memory_space_constraint(v, pltpu.HBM) for v in in_hbm],
        *copied,
        *[pltpu.with_memory_space_constraint(v, VMEM) for v in in_vmem],
    )


def on_device(inputs, w_gate, w_up, out_grads, proj_hidden, proj_model):
    rows, units = inputs.shape[0], w_gate.shape[1]
    par, ex = lax.axis_index("par"), lax.axis_index("ex")
    z_hi, x, core = par // 8, (par // 2) % 4, par % 2

    far = send(inputs, shift_z(4))
    sibling = send(inputs, other_core)
    own, sibling = lax.optimization_barrier((inputs, sibling))
    by_x = [send(own, shift_x(n)) for n in (2, 1, 3)]
    by_x = by_x[1:] + by_x[:1]

    chips = jnp.stack([x, (x + 3) % 4, (x + 1) % 4, (x + 2) % 4])
    cores = jnp.stack([core, 1 - core])
    starts = jnp.stack([z_hi, 1 - z_hi])[:, None, None] * 2048 + chips[:, None] * 512 + cores * 256
    starts = jnp.concatenate([starts.reshape(16), jnp.stack([par, ex])]).astype(jnp.int32)
    w_gate, w_up = w_gate.T, w_up.T
    sums_type, bf16 = ((2 * units, rows), jnp.float32), jnp.bfloat16
    flops = 4 * rows * units * 512
    held, *weights = call(
        stage_kernel,
        "stage",
        [((rows, 256), bf16)] + [((2 * units, 512 * count), bf16) for _, count in PARTS],
        0,
        [starts],
        [],
        [inputs, w_gate, w_up],
        [],
        [],
        [pltpu.SemaphoreType.DMA(()), pltpu.SemaphoreType.DMA((16, 2))],
    )
    far, sibling, held, *weights = lax.optimization_barrier((far, sibling, held, *weights))
    (sums,) = call(own_kernel, "own", [sums_type], flops, [], [], [], [], [held, sibling, weights[0]], [])
    far = [far] + [send(far, shift_x(n)) for n in (1, 3, 2)]
    *by_x, _ = lax.optimization_barrier((*by_x, far[0]))
    near_all = [b for n in by_x for b in (n, send(n, other_core))]
    (sums,) = call(
        near_kernel, "near", [sums_type], 3 * flops, [], [], [], [], [*near_all, weights[1], sums], []
    )
    far[3], sums = lax.optimization_barrier((far[3], sums))
    far_all = [b for n in far for b in (n, send(n, other_core))]
    sums, right = call(
        middle_kernel,
        "middle",
        [sums_type, ((rows, 64), jnp.float32)],
        3 * flops,
        [],
        [],
        [],
        [out_grads, proj_model.T],
        [*far_all[:6], weights[2], sums],
        [],
    )
    (shares,) = call(
        last_kernel,
        "last",
        [((8, 2, SEQ, 128), bf16)],
        flops,
        [],
        [],
        [],
        [proj_hidden.T],
        [*far_all[6:], weights[3], sums, right],
        [VMEM((rows, 128), jnp.float32)],
    )
    shares, par, ex = lax.optimization_barrier((shares, par, ex))

    shares = lax.all_to_all(shares, BOTH, 0, 0, axis_index_groups=SQUARES)
    part = jnp.sum(shares.astype(jnp.float32), axis=0)

    part = jnp.broadcast_to(part.astype(jnp.bfloat16), (8, *part.shape))
    along = lax.all_to_all(part, BOTH, 0, 0, axis_index_groups=LINES).astype(jnp.float32)
    total = (along[:4] + along[4:]).reshape(8, SEQ, 128)
    outer = jnp.einsum("eta,etb->eab", total[..., :64], total[..., 64:], precision=lax.Precision.HIGHEST)
    feats = outer.reshape(8, 4096) / jnp.sqrt(jnp.float32(SEQ))
    features = lax.dynamic_slice_in_dim(feats, ex // 4 * 2 + par // 8, 1, 0)

    feats = jnp.broadcast_to(feats.astype(jnp.bfloat16), (16, 8, 4096))
    feats = lax.all_to_all(feats, BOTH, 0, 0, axis_index_groups=PLANES).reshape(128, 4096)
    feats = jnp.concatenate([feats, send(feats, other_core)])
    mine = lax.dynamic_slice_in_dim(feats, par * 256, 256, 1)
    gram = jnp.dot(mine.T, feats, preferred_element_type=jnp.float32) * (1.0 / 256)
    return (features, gram)


def solution(mesh):
    placed = (
        P("ex", "par"),
        P(None, "par"),
        P(None, "par"),
        P("ex", "par"),
        P("par", None),
        P("par", None),
    )
    return jax.shard_map(
        on_device,
        mesh=mesh,
        in_specs=placed,
        out_specs=(P(("ex", "par"), None), P("par", None)),
        check_vma=False,
    )
```

```python
import functools

import jax
import jax.numpy as jnp
from jax import lax
from jax.experimental import pallas as pl
from jax.experimental.pallas import tpu as pltpu
from jax.sharding import PartitionSpec as P

SEQ = 32
BOTH = ("ex", "par")


def pairs(move):
    def index(z, y, x, core):
        z, y, x = z % 8, y % 4, x % 4
        return ((z % 4) * 4 + y) * 16 + (z // 4) * 8 + x * 2 + core

    return [
        (index(z, y, x, c), index(*move(z, y, x, c)))
        for z in range(8)
        for y in range(4)
        for x in range(4)
        for c in range(2)
    ]


def send(value, move):
    return lax.ppermute(value, BOTH, pairs(move))


def shift_x(n):
    return lambda z, y, x, c: (z, y, x + n, c)


def shift_z(n):
    return lambda z, y, x, c: (z + n, y, x, c)


def other_core(z, y, x, c):
    return (z, y, x, 1 - c)


VMEM = pltpu.VMEM
ROWS_TIMES_ROWS = (((1,), (1,)), ((), ()))
LINES = [[(z % 4 * 4 + y) * 16 + z // 4 * 8 + n for z in range(8)] for y in range(4) for n in range(8)]
SQUARES = [[(z % 4 * 4 + y) * 16 + z // 4 * 8 + n for n in range(8)] for z in range(8) for y in range(4)]
SPIRAL = [(x, (x + y) % 4) for y in range(4) for x in range(4)]
PLANES = [
    [(z % 4 * 4 + y) * 16 + z // 4 * 8 + x * 2 + c for x, y in SPIRAL]
    for z in range(8)
    for c in range(2)
]


PARTS = ((0, 1), (1, 3), (4, 3), (7, 1))


def stage_kernel(starts, inputs, gate, up, held, *refs):
    outs, sem, sems = refs[:4], refs[4], refs[5]
    units = gate.shape[0]
    copies = [pltpu.make_async_copy(inputs, held, sem)]
    for out, (first, count) in zip(outs, PARTS):
        for n in range(2 * count):
            cols = pl.ds(pl.multiple_of(starts[2 * first + n], 256), 256)
            for m, source in enumerate((gate, up)):
                to = out.at[pl.ds(m * units, units), pl.ds(n * 256, 256)]
                copies.append(pltpu.make_async_copy(source.at[:, cols], to, sems.at[2 * first + n, m]))
    for c in copies:
        c.start()
    for c in copies:
        c.wait()


def product(weights, j, first, second):
    held = jnp.concatenate([first[...], second[...]], axis=1)
    cols = weights[:, j * 512 : (j + 1) * 512]
    return lax.dot_general(cols, held, ROWS_TIMES_ROWS, preferred_element_type=jnp.float32)


def own_kernel(first, second, weights, out):
    out[...] = product(weights, 0, first, second)


def three_chips(blocks, weights, near, out):
    out[...] = product(weights, 0, *blocks[:2]) + near[...]
    for j in range(1, 3):
        out[...] += product(weights, j, *blocks[2 * j : 2 * j + 2])


def near_kernel(*refs):
    blocks, (weights, near, out) = refs[:6], refs[6:]
    three_chips(blocks, weights, near, out)


def middle_kernel(grads, proj_model, *refs):
    blocks, (weights, near, out, right) = refs[:6], refs[6:]
    right[...] = lax.dot_general(grads[...], proj_model[...], ROWS_TIMES_ROWS, preferred_element_type=jnp.float32)
    three_chips(blocks, weights, near, out)


def last_kernel(proj, first, second, weights, sums, right, out, whole):
    units = proj.shape[1]
    value = product(weights, 0, first, second) + sums[...]
    gate, up = value[:units], value[units:]
    hidden = (gate / (1.0 + jnp.exp(-gate)) * up).astype(jnp.bfloat16)
    left = jnp.dot(proj[...], hidden, preferred_element_type=jnp.float32)
    whole[:, :64] = left.T
    whole[:, 64:] = right[...]
    for owner in range(8):
        for z_hi in range(2):
            first_row = (z_hi * 8 + owner) * SEQ
            out[owner, z_hi] = whole[first_row : first_row + SEQ].astype(out.dtype)


def call(kernel, name, out, flops, scalars, anywhere, in_hbm, copied, in_vmem, scratch):
    vmem = pl.BlockSpec(memory_space=VMEM)
    return pl.pallas_call(
        kernel,
        out_shape=[VMEM(shape, dtype) for shape, dtype in out],
        in_specs=[pl.BlockSpec(memory_space=pltpu.SMEM)] * len(scalars)
        + [pl.BlockSpec(memory_space=pl.ANY)] * len(anywhere)
        + [pl.BlockSpec(memory_space=pltpu.HBM)] * len(in_hbm)
        + [vmem] * (len(copied) + len(in_vmem)),
        out_specs=[vmem] * len(out),
        scratch_shapes=scratch,
        compiler_params=pltpu.CompilerParams(vmem_limit_bytes=16 * 1024 * 1024),
        cost_estimate=pl.CostEstimate(flops=flops, bytes_accessed=0, transcendentals=0),
        name=name,
    )(
        *scalars,
        *anywhere,
        *[pltpu.with_memory_space_constraint(v, pltpu.HBM) for v in in_hbm],
        *copied,
        *[pltpu.with_memory_space_constraint(v, VMEM) for v in in_vmem],
    )


def on_device(inputs, w_gate, w_up, out_grads, proj_hidden, proj_model):
    rows, units = inputs.shape[0], w_gate.shape[1]
    par, ex = lax.axis_index("par"), lax.axis_index("ex")
    z_hi, x, core = par // 8, (par // 2) % 4, par % 2

    far = send(inputs, shift_z(4))
    sibling = send(inputs, other_core)
    own, sibling = lax.optimization_barrier((inputs, sibling))
    by_x = [send(own, shift_x(n)) for n in (2, 1, 3)]
    by_x = by_x[1:] + by_x[:1]

    chips = jnp.stack([x, (x + 3) % 4, (x + 1) % 4, (x + 2) % 4])
    cores = jnp.stack([core, 1 - core])
    starts = jnp.stack([z_hi, 1 - z_hi])[:, None, None] * 2048 + chips[:, None] * 512 + cores * 256
    starts = jnp.concatenate([starts.reshape(16), jnp.stack([par, ex])]).astype(jnp.int32)
    w_gate, w_up = w_gate.T, w_up.T
    sums_type, bf16 = ((2 * units, rows), jnp.float32), jnp.bfloat16
    flops = 4 * rows * units * 512
    held, *weights = call(
        stage_kernel,
        "stage",
        [((rows, 256), bf16)] + [((2 * units, 512 * count), bf16) for _, count in PARTS],
        0,
        [starts],
        [],
        [inputs, w_gate, w_up],
        [],
        [],
        [pltpu.SemaphoreType.DMA(()), pltpu.SemaphoreType.DMA((16, 2))],
    )
    far, sibling, held, *weights = lax.optimization_barrier((far, sibling, held, *weights))
    (sums,) = call(own_kernel, "own", [sums_type], flops, [], [], [], [], [held, sibling, weights[0]], [])
    far = [far] + [send(far, shift_x(n)) for n in (1, 3, 2)]
    *by_x, _ = lax.optimization_barrier((*by_x, far[0]))
    near_all = [b for n in by_x for b in (n, send(n, other_core))]
    (sums,) = call(
        near_kernel, "near", [sums_type], 3 * flops, [], [], [], [], [*near_all, weights[1], sums], []
    )
    far[3], sums = lax.optimization_barrier((far[3], sums))
    far_all = [b for n in far for b in (n, send(n, other_core))]
    sums, right = call(
        middle_kernel,
        "middle",
        [sums_type, ((rows, 64), jnp.float32)],
        3 * flops,
        [],
        [],
        [],
        [out_grads, proj_model.T],
        [*far_all[:6], weights[2], sums],
        [],
    )
    (shares,) = call(
        last_kernel,
        "last",
        [((8, 2, SEQ, 128), bf16)],
        flops,
        [],
        [],
        [],
        [proj_hidden.T],
        [*far_all[6:], weights[3], sums, right],
        [VMEM((rows, 128), jnp.float32)],
    )
    shares, par, ex = lax.optimization_barrier((shares, par, ex))

    shares = lax.all_to_all(shares, BOTH, 0, 0, axis_index_groups=SQUARES)
    part = jnp.sum(shares.astype(jnp.float32), axis=0)

    part = jnp.broadcast_to(part.astype(jnp.bfloat16), (8, *part.shape))
    along = lax.all_to_all(part, BOTH, 0, 0, axis_index_groups=LINES).astype(jnp.float32)
    total = (along[:4] + along[4:]).reshape(8, SEQ, 128)
    outer = jnp.einsum("eta,etb->eab", total[..., :64], total[..., 64:], precision=lax.Precision.HIGH)
    feats = outer.reshape(8, 4096) / jnp.sqrt(jnp.float32(SEQ))
    features = lax.dynamic_slice_in_dim(feats, ex // 4 * 2 + par // 8, 1, 0)

    feats = jnp.broadcast_to(feats.astype(jnp.bfloat16), (16, 8, 4096))
    feats = lax.all_to_all(feats, BOTH, 0, 0, axis_index_groups=PLANES).reshape(128, 4096)
    feats = jnp.concatenate([feats, send(feats, other_core)])
    mine = lax.dynamic_slice_in_dim(feats, par * 256, 256, 1)
    gram = jnp.dot(mine.T, feats, preferred_element_type=jnp.float32) * (1.0 / 256)
    return (features, gram)


def solution(mesh):
    placed = (
        P("ex", "par"),
        P(None, "par"),
        P(None, "par"),
        P("ex", "par"),
        P("par", None),
        P("par", None),
    )
    return jax.shard_map(
        on_device,
        mesh=mesh,
        in_specs=placed,
        out_specs=(P(("ex", "par"), None), P("par", None)),
        check_vma=False,
    )
```
